32 devices in a mesh: fsdp: 8 (over z, x), context: 4 (over y, core).
Axes of the slice: x: 2, y: 2, z: 4, core: 2. Of those that a mesh axis runs over, the one named last changes fastest.
Arguments:
- block_input: bfloat16 [8, 2048, 1088], P('fsdp', 'context'), may hold values from -6 to 6
- segment_ids: int32 [8, 2048], P('fsdp'), may hold values from 0 to 15, as said below
- ln1_gain: bfloat16 [1088], P('fsdp'), may hold values from 0.099609375 to 1.8984375
- ln1_bias: bfloat16 [1088], P('fsdp'), may hold values from -3 to 3
- w_qkv: bfloat16 [1088, 3264], P('fsdp'), may hold values from -0.1875 to 0.1875
- bias_query: bfloat16 [1088], P('fsdp'), may hold values from -3 to 3
- bias_value: bfloat16 [1088], P('fsdp'), may hold values from -4 to 4
- w_out: bfloat16 [1088, 1088], P('fsdp'), may hold values from -0.75 to 0.75
- bias_out: bfloat16 [1088], P('fsdp'), may hold values from -3 to 3
- ln2_gain: bfloat16 [1088], P('fsdp'), may hold values from 0.099609375 to 1.8984375
- ln2_bias: bfloat16 [1088], P('fsdp'), may hold values from -3 to 3
- w_up: bfloat16 [1088, 4352], P('fsdp'), may hold values from -0.1875 to 0.1875
- bias_up: bfloat16 [4352], P('fsdp'), may hold values from -4 to 4
- w_down: bfloat16 [4352, 1088], P('fsdp'), may hold values from -0.09375 to 0.09375
- bias_down: bfloat16 [1088], P('fsdp'), may hold values from -3 to 3
- cotangent: bfloat16 [8, 2048, 1088], P('fsdp', 'context'), may hold values from -6 to 6
Outputs:
- block_output: bfloat16 [8, 2048, 1088], P('fsdp', 'context')
- input_grad: float32 [8, 2048, 1088], P('fsdp', 'context')
- grad_ln1_gain: float32 [1088], P('fsdp')
- grad_ln1_bias: float32 [1088], P('fsdp')
- grad_w_qkv: float32 [1088, 3264], P('fsdp')
- grad_bias_query: float32 [1088], P('fsdp')
- grad_bias_value: float32 [1088], P('fsdp')
- grad_w_out: float32 [1088, 1088], P('fsdp')
- grad_bias_out: float32 [1088], P('fsdp')
- grad_ln2_gain: float32 [1088], P('fsdp')
- grad_ln2_bias: float32 [1088], P('fsdp')
- grad_w_up: float32 [1088, 4352], P('fsdp')
- grad_bias_up: float32 [4352], P('fsdp')
- grad_w_down: float32 [4352, 1088], P('fsdp')
- grad_bias_down: float32 [1088], P('fsdp')
The draws below stay inside these ranges and needn't reach their ends.
Inputs may be any that keep to these rules, and one draw needn't show every extreme that they name: `segment_ids`: within each sequence the ids never fall; equal ids mark one document, and a token attends only to earlier tokens of its own document.
All inputs are finite; a program needn't handle non-finite values.
Results may differ from the reference program's by a relative error of at most 0.011.
Values may be sent and summed in bfloat16 or wider, within the bound.
A program may use at most 384 MiB of HBM per device.

```python
import jax
import jax.numpy as jnp
from jax import lax

D = 1088
HEAD_DIM = 64
FF = 4352
LENGTH = 2048
STRETCH = 512
SEQS = 1
TOTAL_SEQS = 8


def draw_segment_ids(key, part):
    key = jax.random.fold_in(key, 5)
    key_len, key_pick, key_start, key_finish = jax.random.split(key, 4)
    doc_lengths = jax.random.randint(key_len, (TOTAL_SEQS, 16), max(LENGTH // 10, 1), LENGTH + 1)
    doc_ends = jnp.cumsum(doc_lengths, axis=1)
    places = jnp.arange(LENGTH, dtype=jnp.int32)
    general = jnp.sum((doc_ends[:, None, :] <= places[None, :, None]).astype(jnp.int32), axis=2)
    picked = jax.random.randint(key_pick, (TOTAL_SEQS // SEQS,), 0, SEQS)
    chosen_row = jnp.arange(TOTAL_SEQS, dtype=jnp.int32) % SEQS == jnp.repeat(picked, SEQS)
    start_at = jax.random.randint(key_start, (TOTAL_SEQS,), 0, STRETCH)
    finish_at = jax.random.randint(key_finish, (TOTAL_SEQS,), LENGTH - STRETCH + 1, LENGTH)
    middle_doc = (places[None, :] >= start_at[:, None]).astype(jnp.int32)
    special = jnp.where(places[None, :] >= finish_at[:, None], 15, middle_doc)
    return jnp.where(chosen_row[:, None], special, general).astype(jnp.int32)


def block_scale(rng, shape, pieces, least, high):
    loudness, own = 1.0, jax.random.fold_in(rng, 6)
    for axis_at, shards_of in pieces:
        steps = jnp.exp(jax.random.uniform(jax.random.fold_in(own, axis_at), (shards_of,), jnp.float32, least / len(pieces), high / len(pieces)))
        loudness = loudness * jnp.repeat(steps, shape[axis_at] // shards_of).reshape([-1 if axis == axis_at else 1 for axis in range(len(shape))])
    return loudness


def normal_values(own_key, dims, deviation, most, shards=(), kind=jnp.bfloat16):
    drawn = jax.random.normal(own_key, dims, jnp.float32) * deviation
    if len(shards) > 0:
        drawn = block_scale(own_key, dims, shards, -0.22, 0.18) * drawn
    return jnp.clip(drawn, min=-most, max=most).astype(kind)


def setup_inputs(seed: int = 0) -> dict:
    arg_keys = jax.random.split(jax.random.key(seed), 17)
    return {
        "block_input": normal_values(arg_keys[0], (TOTAL_SEQS, LENGTH, D), 1.0, 6.0, ((0, 8), (1, 4))),
        "segment_ids": draw_segment_ids(jax.random.fold_in(arg_keys[16], 71), 0),
        "ln1_gain": jnp.clip(1.0 + 0.18 * jax.random.normal(arg_keys[2], (D,), jnp.float32), 0.099609375, 1.8984375).astype(jnp.bfloat16),
        "ln1_bias": normal_values(arg_keys[3], (D,), 0.3, 3.0, ((0, 8),)),
        "w_qkv": normal_values(arg_keys[4], (D, 3 * D), D ** -0.5, 0.1875, ((0, 8),)),
        "bias_query": normal_values(arg_keys[5], (D,), 0.3, 3.0, ((0, 8),)),
        "bias_value": normal_values(arg_keys[6], (D,), 0.5, 4.0, ((0, 8),)),
        "w_out": normal_values(arg_keys[7], (D, D), (D // 16) ** -0.5, 0.75, ((0, 8),)),
        "bias_out": normal_values(arg_keys[8], (D,), 0.3, 3.0, ((0, 8),)),
        "ln2_gain": jnp.clip(1.0 + 0.18 * jax.random.normal(arg_keys[9], (D,), jnp.float32), 0.099609375, 1.8984375).astype(jnp.bfloat16),
        "ln2_bias": normal_values(arg_keys[10], (D,), 0.3, 3.0, ((0, 8),)),
        "w_up": normal_values(arg_keys[11], (D, FF), D ** -0.5, 0.1875, ((0, 8),)),
        "bias_up": normal_values(arg_keys[12], (FF,), 0.5, 4.0, ((0, 8),)),
        "w_down": normal_values(arg_keys[13], (FF, D), FF ** -0.5, 0.09375, ((0, 8),)),
        "bias_down": normal_values(arg_keys[14], (D,), 0.3, 3.0, ((0, 8),)),
        "cotangent": normal_values(arg_keys[15], (TOTAL_SEQS, LENGTH, D), 1.0, 6.0, ((0, 8), (1, 4))),
    }


@jax.custom_vjp
def low(v):
    return lax.optimization_barrier(v.astype(jnp.bfloat16)).astype(jnp.float32)

@jax.custom_vjp
def low_back(v):
    return v

def low_keep(v):
    return (low(v), None)

def low_pass(kept, grad):
    return (grad,)

def back_keep(v):
    return (v, None)

def back_low(kept, grad):
    return (low(grad),)
low.defvjp(low_keep, low_pass)
low_back.defvjp(back_keep, back_low)
exactly = lax.Precision.HIGHEST
masked_score = -1e+30

def normalize(inputs, scale_vec, shift_vec):
    average = lax.optimization_barrier(jnp.mean(inputs, axis=-1, keepdims=True))
    centered = inputs - average
    variance = lax.optimization_barrier(jnp.mean(centered * centered, axis=-1, keepdims=True))
    return centered * lax.rsqrt(variance + 1e-05) * scale_vec + shift_vec

def attend(queries, keys, values, segments):
    head_count = D // HEAD_DIM
    block_rows = min(512, LENGTH)
    blocks = LENGTH // block_rows
    key_heads = keys.reshape(LENGTH, head_count, HEAD_DIM)
    value_heads = values.reshape(LENGTH, head_count, HEAD_DIM)
    query_blocks = queries.reshape(blocks, block_rows, head_count, HEAD_DIM)
    starts = jnp.arange(blocks, dtype=jnp.int32) * block_rows
    key_place = jnp.arange(LENGTH, dtype=jnp.int32)

    @jax.checkpoint
    def one_block(item):
        query_block, start = item
        query_place = start + jnp.arange(block_rows, dtype=jnp.int32)
        query_segs = lax.dynamic_slice_in_dim(segments, start, block_rows, 0)
        raw = jnp.einsum('qhd,khd->hqk', query_block, key_heads, precision=exactly) * 0.125
        allowed = (key_place[None, :] <= query_place[:, None]) & (segments[None, :] == query_segs[:, None])
        scores = low_back(jnp.where(allowed[None], raw, masked_score))
        largest = lax.optimization_barrier(jnp.max(scores, axis=-1, keepdims=True))
        weights = jnp.exp(scores - largest)
        probs = weights / lax.optimization_barrier(jnp.sum(weights, axis=-1, keepdims=True))
        mixed = jnp.einsum('hqk,khd->qhd', low(probs), value_heads, precision=exactly)
        return mixed.reshape(block_rows, D)
    return lax.map(one_block, (query_blocks, starts)).reshape(LENGTH, D)

def layer(params, inputs, segments):
    gain_one, shift_one, proj_qkv, query_bias, value_bias, proj_out, out_bias, gain_two, shift_two, proj_up, up_bias, proj_down, down_bias = params
    normed = low(normalize(inputs, gain_one, shift_one))
    stacked = jnp.dot(normed, proj_qkv, precision=exactly)
    queries = low(low_back(stacked[:, :D] + query_bias))
    keys = low(low_back(stacked[:, D:2 * D]))
    values = low(low_back(stacked[:, 2 * D:] + value_bias))
    attended = low(low_back(attend(queries, keys, values, segments)))
    middle = inputs + low_back(jnp.dot(attended, proj_out, precision=exactly) + out_bias)
    normed_two = low(normalize(middle, gain_two, shift_two))
    pre_act = low_back(jnp.dot(normed_two, proj_up, precision=exactly) + up_bias)
    hidden = low(jax.nn.gelu(pre_act, approximate=True))
    return middle + jnp.dot(hidden, proj_down, precision=exactly) + down_bias

def reference(block_input, segment_ids, ln1_gain, ln1_bias, w_qkv, bias_query, bias_value, w_out, bias_out, ln2_gain, ln2_bias, w_up, bias_up, w_down, bias_down, cotangent):
    params = tuple((element.astype(jnp.float32) for element in (ln1_gain, ln1_bias, w_qkv, bias_query, bias_value, w_out, bias_out, ln2_gain, ln2_bias, w_up, bias_up, w_down, bias_down)))

    def one_sequence(totals, item):
        inputs, segments, grad_out = item

        def forward(weights, acts):
            return layer(weights, acts, segments)
        result, pull = jax.vjp(forward, params, inputs.astype(jnp.float32))
        grad_params, grad_inputs = pull(grad_out.astype(jnp.float32))
        totals = jax.tree.map(lambda total, extra: total + extra, totals, grad_params)
        return (totals, (result.astype(jnp.bfloat16), grad_inputs))
    zeros = jax.tree.map(jnp.zeros_like, params)
    grads, (outputs, input_grads) = lax.scan(one_sequence, zeros, (block_input, segment_ids, cotangent))
    return (outputs, input_grads, grads[0], grads[1], grads[2], grads[3], grads[4], grads[5], grads[6], grads[7], grads[8], grads[9], grads[10], grads[11], grads[12])
```

```python
import jax
import jax.numpy as jnp
from jax import lax
from jax.sharding import PartitionSpec as P

HEAD_DIM = 64


masked_score = -1e30


def normalize(inputs, scale_vec, shift_vec):
    average = jnp.mean(inputs, axis=-1, keepdims=True)
    centered = inputs - average
    variance = jnp.mean(centered * centered, axis=-1, keepdims=True)
    return centered * lax.rsqrt(variance + 1e-05) * scale_vec + shift_vec


def gelu_tanh(pre_act):
    return jax.nn.gelu(pre_act, approximate=True)


def contract_rows(left, right):
    return lax.dot_general(
        left, right, (((0,), (0,)), ((), ())), preferred_element_type=jnp.float32
    )


def contract_cols(left, right):
    return lax.dot_general(
        left, right, (((1,), (1,)), ((), ())), preferred_element_type=jnp.float32
    )

class Links:
    def __init__(self):
        self.shards = lax.axis_size("fsdp")
        self.places = lax.axis_size("context")
        self.depth = self.shards // 2
        self.shard = lax.axis_index("fsdp")
        self.place = lax.axis_index("context")
        self.z = self.shard // 2
        self.x = self.shard % 2
        self.core = self.place % 2
        self.even = (self.place // 2) % 2 == 0

    def swap(self, value, axis, bit):
        count = lax.axis_size(axis)
        return lax.ppermute(value, axis, [(i, i ^ bit) for i in range(count)])

    def right(self, value, distance):
        pairs = []
        for z in range(self.depth - 1):
            if z + 1 >= distance:
                pairs += [(2 * z, 2 * z + 2), (2 * z + 1, 2 * z + 3)]
        return lax.ppermute(value, "fsdp", pairs)

    def left(self, value, distance):
        pairs = []
        for z in range(1, self.depth):
            if z - 1 + distance < self.depth:
                pairs += [(2 * z, 2 * z - 2), (2 * z + 1, 2 * z - 1)]
        return lax.ppermute(value, "fsdp", pairs)

    def block_at(self, k):
        return lax.rem(self.z + k, self.depth)

    def gather_pairs(self, mine):
        rights, lefts = [mine], [mine]
        for distance in range(1, self.depth):
            rights.append(self.right(rights[-1], distance))
            lefts.append(self.left(lefts[-1], distance))
        pairs = []
        for k in range(self.depth):
            if k == 0:
                block = mine
            else:
                block = jnp.where(self.z + k < self.depth, lefts[k], rights[self.depth - k])
            other = self.swap(block, "fsdp", 1)
            pairs.append(
                jnp.stack(
                    [jnp.where(self.x == 0, block, other), jnp.where(self.x == 0, other, block)]
                )
            )
        return pairs

    def reduce_line(self, blocks):
        from_left, from_right = None, None
        for distance in range(self.depth - 1, 0, -1):
            going_right = blocks[distance].astype(jnp.float32)
            going_left = blocks[self.depth - distance].astype(jnp.float32)
            if from_left is not None:
                going_right = going_right + from_left.astype(jnp.float32)
                going_left = going_left + from_right.astype(jnp.float32)
            right_pairs, left_pairs = [], []
            for z in range(self.depth - distance):
                right_pairs += [(2 * z, 2 * z + 2), (2 * z + 1, 2 * z + 3)]
            for z in range(distance, self.depth):
                left_pairs += [(2 * z, 2 * z - 2), (2 * z + 1, 2 * z - 1)]
            from_left = lax.ppermute(going_right.astype(jnp.bfloat16), "fsdp", right_pairs)
            from_right = lax.ppermute(going_left.astype(jnp.bfloat16), "fsdp", left_pairs)
        total = blocks[0].astype(jnp.float32)
        if from_left is not None:
            total = total + from_left.astype(jnp.float32) + from_right.astype(jnp.float32)
        return total

    def sum_same_parity(self, value):
        bit = 4
        while bit < self.places:
            value = add_low(value, self.swap(value, "context", bit))
            bit *= 2
        return value


def add_low(left, right):
    return (left.astype(jnp.float32) + right.astype(jnp.float32)).astype(jnp.bfloat16)


def set_at(buffer, block, *at):
    at = at + (0,) * (buffer.ndim - len(at))
    return lax.dynamic_update_slice(buffer, block, tuple(jnp.asarray(i, jnp.int32) for i in at))


def quarters(shard, features):
    return jnp.stack([shard[:, j * features : (j + 1) * features] for j in range(4)])


def gather_first(links, w_qkv, w_out):
    rows, features = w_out.shape
    own = quarters(jnp.concatenate([w_qkv, w_out], axis=1), features)
    mine = lax.dynamic_slice_in_dim(own, 2 * links.core, 2, 0)
    full = jnp.zeros((4, links.shards, rows, features), jnp.bfloat16)
    for k, pair in enumerate(links.gather_pairs(mine)):
        block = pair.transpose(1, 0, 2, 3)
        other = links.swap(block, "context", 1)
        at = 2 * links.block_at(k)
        full = set_at(full, block, 2 * links.core, at)
        full = set_at(full, other, 2 - 2 * links.core, at)
    return full.reshape(4, links.shards * rows, features)


def gather_second(links, w_up, w_down):
    rows = w_up.shape[0]
    features = w_down.shape[1]
    own_up = lax.dynamic_slice_in_dim(quarters(w_up, features), 2 * links.core, 2, 0)
    own_down = lax.dynamic_index_in_dim(
        w_down.reshape(2, 2, rows, features), links.core, 0, keepdims=False
    )
    mine = jnp.where(links.even, own_up, own_down)
    up = jnp.zeros((4, links.shards, rows, features), jnp.bfloat16)
    down = jnp.zeros((links.shards, 2, 2, rows, features), jnp.bfloat16)
    for k, pair in enumerate(links.gather_pairs(mine)):
        other = links.swap(pair, "context", 2)
        up_half = jnp.where(links.even, pair, other).transpose(1, 0, 2, 3)
        down_half = jnp.where(links.even, other, pair)
        up_other = links.swap(up_half, "context", 1)
        down_other = links.swap(down_half, "context", 1)
        at = 2 * links.block_at(k)
        up = set_at(up, up_half, 2 * links.core, at)
        up = set_at(up, up_other, 2 - 2 * links.core, at)
        down = set_at(down, down_half[:, None], at, links.core)
        down = set_at(down, down_other[:, None], at, 1 - links.core)
    return (
        up.reshape(4, links.shards * rows, features),
        down.reshape(4 * links.shards * rows, features),
    )


def other_x(links, block):
    sent = lax.dynamic_index_in_dim(block, 1 - links.x, 0, keepdims=False)
    kept = lax.dynamic_index_in_dim(block, links.x, 0, keepdims=False)
    return add_low(kept, links.swap(sent, "fsdp", 1))


def reduce_second(links, grad_up, grad_down):
    features = grad_down.shape[1]
    rows = features // links.shards
    up = grad_up.reshape(2, 2, links.depth, 2, rows, features)
    down = grad_down.reshape(links.depth, 2, 2, 2, rows, features)
    blocks = []
    for k in range(links.depth):
        at = links.block_at(k)
        up_k = lax.dynamic_index_in_dim(up, at, 2, keepdims=False).transpose(0, 2, 1, 3, 4)
        down_k = lax.dynamic_index_in_dim(down, at, 0, keepdims=False).transpose(1, 0, 2, 3, 4)
        both = jnp.stack([up_k, down_k])
        sent = lax.dynamic_index_in_dim(both, 1 - links.core, 1, keepdims=False)
        kept = lax.dynamic_index_in_dim(both, links.core, 1, keepdims=False)
        halves = add_low(kept, links.swap(sent, "context", 1))
        sent = jnp.where(links.even, halves[1], halves[0])
        kept = jnp.where(links.even, halves[0], halves[1])
        block = add_low(kept, links.swap(sent, "context", 2))
        block = links.sum_same_parity(block)
        blocks.append(other_x(links, block))
    mine = links.reduce_line(blocks).astype(jnp.bfloat16)
    other = links.swap(mine, "context", 2)
    up_half = jnp.where(links.even, mine, other)
    down_half = jnp.where(links.even, other, mine)
    both = jnp.stack([up_half, down_half])
    return join_cores(links, both)


def join_cores(links, half):
    other = links.swap(half, "context", 1)
    first = jnp.where(links.core == 0, half, other)
    last = jnp.where(links.core == 0, other, half)
    return jnp.concatenate([first, last], axis=-3).astype(jnp.float32)


def reduce_first(links, grads):
    features = grads.shape[1]
    rows = features // links.shards
    split = grads.reshape(2, 2, links.depth, 2, rows, features)
    blocks = []
    for k in range(links.depth):
        part = lax.dynamic_index_in_dim(split, links.block_at(k), 2, keepdims=False)
        part = part.transpose(0, 2, 1, 3, 4)
        sent = lax.dynamic_index_in_dim(part, 1 - links.core, 0, keepdims=False)
        kept = lax.dynamic_index_in_dim(part, links.core, 0, keepdims=False)
        blocks.append(other_x(links, add_low(kept, links.swap(sent, "context", 1))))
    mine = links.reduce_line(blocks).astype(jnp.bfloat16)
    mine = add_low(mine, links.swap(mine, "context", 2))
    mine = links.sum_same_parity(mine)
    return join_cores(links, mine)


def sum_everywhere(links, value):
    for axis, count in (("context", links.places), ("fsdp", links.shards)):
        bit = 1
        while bit < count:
            value = value + links.swap(value, axis, bit)
            bit *= 2
    return value


def score_table(query_rows, key_rows, query_segs, key_segs, query_place, key_place, head_count):
    query_heads = query_rows.reshape(query_rows.shape[0], head_count, HEAD_DIM)
    key_heads = key_rows.reshape(key_rows.shape[0], head_count, HEAD_DIM)
    raw = (
        jnp.einsum("qhd,khd->hqk", query_heads, key_heads, preferred_element_type=jnp.float32)
        * 0.125
    )
    allowed = (key_place[None, :] <= query_place[:, None]) & (
        key_segs[None, :] == query_segs[:, None]
    )
    return jnp.where(allowed[None], raw, masked_score)


def local(
    block_input,
    segment_ids,
    ln1_gain,
    ln1_bias,
    w_qkv,
    bias_query,
    bias_value,
    w_out,
    bias_out,
    ln2_gain,
    ln2_bias,
    w_up,
    bias_up,
    w_down,
    bias_down,
    cotangent,
):
    sequences, stretch, features = block_input.shape
    head_count = features // HEAD_DIM
    length_all = stretch * lax.axis_size("context")
    offset = lax.axis_index("context") * stretch
    tokens = sequences * stretch
    links = Links()
    small = (
        ln1_gain, ln1_bias, bias_query, bias_value, bias_out, ln2_gain, ln2_bias, bias_down, bias_up
    )
    small_all = lax.all_gather(jnp.concatenate(small), "fsdp", axis=0)
    small_full, start = [], 0
    for vector in small:
        small_full.append(small_all[:, start : start + vector.shape[0]].reshape(-1))
        start += vector.shape[0]
    (
        gain_one,
        shift_one,
        query_bias,
        value_bias,
        out_bias,
        gain_two,
        shift_two,
        down_bias,
        up_bias,
    ) = small_full
    full_first = gather_first(links, w_qkv, w_out)
    full_up, full_down = gather_second(links, w_up, w_down)
    full_out = full_first[3]
    gain_one = gain_one.astype(jnp.float32)
    shift_one = shift_one.astype(jnp.float32)
    gain_two = gain_two.astype(jnp.float32)
    shift_two = shift_two.astype(jnp.float32)
    inputs = block_input.reshape(tokens, features).astype(jnp.float32)
    normed = normalize(inputs, gain_one, shift_one).astype(jnp.bfloat16)
    queries, keys_own, values_own = (
        jnp.dot(normed, full_first[j], preferred_element_type=jnp.float32) for j in range(3)
    )
    queries = (queries + query_bias.astype(jnp.float32)).astype(jnp.bfloat16)
    keys_own = keys_own.astype(jnp.bfloat16)
    values_own = (values_own + value_bias.astype(jnp.float32)).astype(jnp.bfloat16)
    query_seqs = queries.reshape(sequences, stretch, features)
    key_seqs = keys_own.reshape(sequences, stretch, features)
    value_seqs = values_own.reshape(sequences, stretch, features)
    keys_all, values_all = (
        lax.all_gather(key_seqs, "context", axis=1, tiled=True),
        lax.all_gather(value_seqs, "context", axis=1, tiled=True),
    )
    query_place = offset + jnp.arange(stretch, dtype=jnp.int32)
    key_place = jnp.arange(length_all, dtype=jnp.int32)
    own_segs = lax.dynamic_slice_in_dim(segment_ids, offset, stretch, 1)

    def forward_one(item):
        query_rows, key_rows, value_rows, segs_own, segs_all = item
        scores = score_table(
            query_rows, key_rows, segs_own, segs_all, query_place, key_place, head_count
        )
        largest = jnp.max(scores, axis=-1, keepdims=True)
        weights = jnp.exp(scores - largest)
        totals = jnp.sum(weights, axis=-1, keepdims=True)
        probs = (weights / totals).astype(jnp.bfloat16)
        value_heads = value_rows.reshape(length_all, head_count, HEAD_DIM)
        mixed = jnp.einsum("hqk,khd->qhd", probs, value_heads, preferred_element_type=jnp.float32)
        lse_rows = largest[:, :, 0] + jnp.log(totals[:, :, 0])
        return (mixed.reshape(stretch, features).astype(jnp.bfloat16), lse_rows)

    attended, lse_kept = lax.map(
        forward_one, (query_seqs, keys_all, values_all, own_segs, segment_ids)
    )
    attended = attended.reshape(tokens, features)
    middle = (
        inputs
        + jnp.dot(attended, full_out, preferred_element_type=jnp.float32)
        + out_bias.astype(jnp.float32)
    )
    normed_two = normalize(middle, gain_two, shift_two).astype(jnp.bfloat16)
    pre_act = jnp.concatenate(
        [jnp.dot(normed_two, full_up[j], preferred_element_type=jnp.float32) for j in range(4)],
        axis=1,
    ) + up_bias.astype(jnp.float32)
    hidden = gelu_tanh(pre_act).astype(jnp.bfloat16)
    result = (
        middle
        + jnp.dot(hidden, full_down, preferred_element_type=jnp.float32)
        + down_bias.astype(jnp.float32)
    )
    block_output = result.astype(jnp.bfloat16).reshape(block_input.shape)
    grad_out = cotangent.reshape(tokens, features)
    grad_out_f = grad_out.astype(jnp.float32)
    grad_w_down = contract_rows(hidden, grad_out).astype(jnp.bfloat16)
    grad_b_down = jnp.sum(grad_out_f, axis=0)
    grad_hidden = contract_cols(grad_out, full_down)
    gelu_value, gelu_pull = jax.vjp(gelu_tanh, pre_act)
    grad_pre = gelu_pull(grad_hidden)[0].astype(jnp.bfloat16)
    grad_w_up = jnp.stack(
        [
            contract_rows(normed_two, grad_pre[:, j * features : (j + 1) * features])
            for j in range(4)
        ]
    ).astype(jnp.bfloat16)
    second_sums = reduce_second(links, grad_w_up, grad_w_down)
    grad_b_up = jnp.sum(grad_pre.astype(jnp.float32), axis=0)
    grad_normed_two = sum(
        contract_cols(grad_pre[:, j * features : (j + 1) * features], full_up[j]) for j in range(4)
    )
    norm_value, norm_pull = jax.vjp(normalize, middle, gain_two, shift_two)
    grad_middle_part, grad_gain_two, grad_shift_two = norm_pull(grad_normed_two)
    grad_middle = grad_out_f + grad_middle_part
    grad_middle_low = grad_middle.astype(jnp.bfloat16)
    grad_w_out = contract_rows(attended, grad_middle_low)
    grad_b_out = jnp.sum(grad_middle_low.astype(jnp.float32), axis=0)
    grad_attended = contract_cols(grad_middle_low, full_out).astype(jnp.bfloat16)
    grad_att_seqs = grad_attended.reshape(sequences, stretch, features)

    def local_grads(item):
        query_rows, key_rows, value_rows, grad_rows, segs_own, segs_all, lse_rows = item
        scores = score_table(
            query_rows, key_rows, segs_own, segs_all, query_place, key_place, head_count
        )
        probs = jnp.exp(scores - lse_rows[:, :, None])
        grad_heads = grad_rows.reshape(stretch, head_count, HEAD_DIM)
        value_heads = value_rows.reshape(length_all, head_count, HEAD_DIM)
        key_heads = key_rows.reshape(length_all, head_count, HEAD_DIM)
        grad_probs = jnp.einsum(
            "qhd,khd->hqk", grad_heads, value_heads, preferred_element_type=jnp.float32
        )
        deltas = jnp.sum(probs * grad_probs, axis=-1)
        grad_scores = (probs * (grad_probs - deltas[:, :, None])).astype(jnp.bfloat16)
        grad_query = (
            jnp.einsum(
                "hqk,khd->qhd", grad_scores, key_heads, preferred_element_type=jnp.float32
            ).reshape(stretch, features)
            * 0.125
        )
        query_heads = query_rows.reshape(stretch, head_count, HEAD_DIM)
        key_part = (
            jnp.einsum(
                "hqk,qhd->khd", grad_scores, query_heads, preferred_element_type=jnp.float32
            ).reshape(length_all, features)
            * 0.125
        )
        value_part = jnp.einsum(
            "hqk,qhd->khd",
            probs.astype(jnp.bfloat16),
            grad_heads,
            preferred_element_type=jnp.float32,
        ).reshape(length_all, features)
        return (grad_query, key_part.astype(jnp.bfloat16), value_part.astype(jnp.bfloat16))

    local_items = (query_seqs, keys_all, values_all, grad_att_seqs, own_segs, segment_ids, lse_kept)
    grad_queries, key_parts, value_parts = lax.map(local_grads, local_items)
    grad_keys, grad_values = (
        lax.psum_scatter(key_parts, "context", scatter_dimension=1, tiled=True),
        lax.psum_scatter(value_parts, "context", scatter_dimension=1, tiled=True),
    )
    grad_queries = grad_queries.reshape(tokens, features).astype(jnp.bfloat16)
    grad_keys = grad_keys.reshape(tokens, features).astype(jnp.bfloat16)
    grad_values = grad_values.reshape(tokens, features).astype(jnp.bfloat16)
    grads_first = jnp.stack(
        [contract_rows(normed, part) for part in (grad_queries, grad_keys, grad_values)]
        + [grad_w_out]
    ).astype(jnp.bfloat16)
    first_sums = reduce_first(links, grads_first)
    grad_b_query = jnp.sum(grad_queries.astype(jnp.float32), axis=0)
    grad_b_value = jnp.sum(grad_values.astype(jnp.float32), axis=0)
    grad_normed = (
        contract_cols(grad_queries, full_first[0])
        + contract_cols(grad_keys, full_first[1])
        + contract_cols(grad_values, full_first[2])
    )
    first_value, first_pull = jax.vjp(normalize, inputs, gain_one, shift_one)
    grad_input_part, grad_gain_one, grad_shift_one = first_pull(grad_normed)
    input_grad = (grad_middle + grad_input_part).reshape(block_input.shape)
    vectors = (
        grad_gain_one,
        grad_shift_one,
        grad_b_query,
        grad_b_value,
        grad_b_out,
        grad_gain_two,
        grad_shift_two,
        grad_b_down,
        grad_b_up,
    )
    vector_sums = sum_everywhere(links, jnp.concatenate(vectors))
    mine, start = [], 0
    for vector in vectors:
        size = vector.shape[0]
        own = size // links.shards
        mine.append(lax.dynamic_slice_in_dim(vector_sums, start + links.shard * own, own, 0))
        start += size
    up_sum, down_sum = second_sums[0], second_sums[1]
    return (
        block_output,
        input_grad,
        mine[0],
        mine[1],
        jnp.concatenate([first_sums[j] for j in range(3)], axis=1),
        mine[2],
        mine[3],
        first_sums[3],
        mine[4],
        mine[5],
        mine[6],
        jnp.concatenate([up_sum[j] for j in range(4)], axis=1),
        mine[8],
        down_sum.reshape(-1, features),
        mine[7],
    )


def solution(mesh):
    in_specs = (
        P("fsdp", "context", None),
        P("fsdp", None),
        P("fsdp"),
        P("fsdp"),
        P("fsdp", None),
        P("fsdp"),
        P("fsdp"),
        P("fsdp", None),
        P("fsdp"),
        P("fsdp"),
        P("fsdp"),
        P("fsdp", None),
        P("fsdp"),
        P("fsdp", None),
        P("fsdp"),
        P("fsdp", "context", None),
    )
    out_specs = (
        P("fsdp", "context", None),
        P("fsdp", "context", None),
        P("fsdp"),
        P("fsdp"),
        P("fsdp", None),
        P("fsdp"),
        P("fsdp"),
        P("fsdp", None),
        P("fsdp"),
        P("fsdp"),
        P("fsdp"),
        P("fsdp", None),
        P("fsdp"),
        P("fsdp", None),
        P("fsdp"),
    )
    return jax.shard_map(local, mesh=mesh, in_specs=in_specs, out_specs=out_specs, check_vma=False)
```

```python
import functools

import jax
import jax.numpy as jnp
from jax import lax
from jax.experimental import pallas as pl
from jax.experimental.pallas import tpu as pltpu
from jax.sharding import PartitionSpec as P

HEAD_DIM = 64


masked_score = -1e30


def normalize(inputs, scale_vec, shift_vec):
    average = jnp.mean(inputs, axis=-1, keepdims=True)
    centered = inputs - average
    variance = jnp.mean(centered * centered, axis=-1, keepdims=True)
    return centered * lax.rsqrt(variance + 1e-05) * scale_vec + shift_vec


def gelu_tanh(pre_act):
    return jax.nn.gelu(pre_act, approximate=True)


def contract_rows(left, right):
    return lax.dot_general(
        left, right, (((0,), (0,)), ((), ())), preferred_element_type=jnp.float32
    )


def contract_cols(left, right):
    return lax.dot_general(
        left, right, (((1,), (1,)), ((), ())), preferred_element_type=jnp.float32
    )

class Links:
    def __init__(self):
        self.shards = lax.axis_size("fsdp")
        self.places = lax.axis_size("context")
        self.depth = self.shards // 2
        self.shard = lax.axis_index("fsdp")
        self.place = lax.axis_index("context")
        self.z = self.shard // 2
        self.x = self.shard % 2
        self.core = self.place % 2
        self.even = (self.place // 2) % 2 == 0

    def swap(self, value, axis, bit):
        count = lax.axis_size(axis)
        return lax.ppermute(value, axis, [(i, i ^ bit) for i in range(count)])

    def right(self, value, distance):
        pairs = []
        for z in range(self.depth - 1):
            if z + 1 >= distance:
                pairs += [(2 * z, 2 * z + 2), (2 * z + 1, 2 * z + 3)]
        return lax.ppermute(value, "fsdp", pairs)

    def left(self, value, distance):
        pairs = []
        for z in range(1, self.depth):
            if z - 1 + distance < self.depth:
                pairs += [(2 * z, 2 * z - 2), (2 * z + 1, 2 * z - 1)]
        return lax.ppermute(value, "fsdp", pairs)

    def block_at(self, k):
        return lax.rem(self.z + k, self.depth)

    def gather_pairs(self, mine):
        rights, lefts = [mine], [mine]
        for distance in range(1, self.depth):
            rights.append(self.right(rights[-1], distance))
            lefts.append(self.left(lefts[-1], distance))
        pairs = []
        for k in range(self.depth):
            if k == 0:
                block = mine
            else:
                block = jnp.where(self.z + k < self.depth, lefts[k], rights[self.depth - k])
            other = self.swap(block, "fsdp", 1)
            pairs.append(
                jnp.stack(
                    [jnp.where(self.x == 0, block, other), jnp.where(self.x == 0, other, block)]
                )
            )
        return pairs

    def reduce_line(self, blocks):
        from_left, from_right = None, None
        for distance in range(self.depth - 1, 0, -1):
            going_right = blocks[distance].astype(jnp.float32)
            going_left = blocks[self.depth - distance].astype(jnp.float32)
            if from_left is not None:
                going_right = going_right + from_left.astype(jnp.float32)
                going_left = going_left + from_right.astype(jnp.float32)
            right_pairs, left_pairs = [], []
            for z in range(self.depth - distance):
                right_pairs += [(2 * z, 2 * z + 2), (2 * z + 1, 2 * z + 3)]
            for z in range(distance, self.depth):
                left_pairs += [(2 * z, 2 * z - 2), (2 * z + 1, 2 * z - 1)]
            from_left = lax.ppermute(going_right.astype(jnp.bfloat16), "fsdp", right_pairs)
            from_right = lax.ppermute(going_left.astype(jnp.bfloat16), "fsdp", left_pairs)
        total = blocks[0].astype(jnp.float32)
        if from_left is not None:
            total = total + from_left.astype(jnp.float32) + from_right.astype(jnp.float32)
        return total

    def sum_same_parity(self, value):
        bit = 4
        while bit < self.places:
            value = add_low(value, self.swap(value, "context", bit))
            bit *= 2
        return value


def add_low(left, right):
    return (left.astype(jnp.float32) + right.astype(jnp.float32)).astype(jnp.bfloat16)


def set_at(buffer, block, *at):
    at = at + (0,) * (buffer.ndim - len(at))
    return lax.dynamic_update_slice(buffer, block, tuple(jnp.asarray(i, jnp.int32) for i in at))


def quarters(shard, features):
    return jnp.stack([shard[:, j * features : (j + 1) * features] for j in range(4)])


def gather_first(links, w_qkv, w_out):
    rows, features = w_out.shape
    own = quarters(jnp.concatenate([w_qkv, w_out], axis=1), features)
    mine = lax.dynamic_slice_in_dim(own, 2 * links.core, 2, 0)
    full = jnp.zeros((4, links.shards, rows, features), jnp.bfloat16)
    for k, pair in enumerate(links.gather_pairs(mine)):
        block = pair.transpose(1, 0, 2, 3)
        other = links.swap(block, "context", 1)
        at = 2 * links.block_at(k)
        full = set_at(full, block, 2 * links.core, at)
        full = set_at(full, other, 2 - 2 * links.core, at)
    return full.reshape(4, links.shards * rows, features)


def gather_second(links, w_up, w_down):
    rows = w_up.shape[0]
    features = w_down.shape[1]
    own_up = lax.dynamic_slice_in_dim(quarters(w_up, features), 2 * links.core, 2, 0)
    own_down = lax.dynamic_index_in_dim(
        w_down.reshape(2, 2, rows, features), links.core, 0, keepdims=False
    )
    mine = jnp.where(links.even, own_up, own_down)
    up = jnp.zeros((4, links.shards, rows, features), jnp.bfloat16)
    down = jnp.zeros((links.shards, 2, 2, rows, features), jnp.bfloat16)
    for k, pair in enumerate(links.gather_pairs(mine)):
        other = links.swap(pair, "context", 2)
        up_half = jnp.where(links.even, pair, other).transpose(1, 0, 2, 3)
        down_half = jnp.where(links.even, other, pair)
        up_other = links.swap(up_half, "context", 1)
        down_other = links.swap(down_half, "context", 1)
        at = 2 * links.block_at(k)
        up = set_at(up, up_half, 2 * links.core, at)
        up = set_at(up, up_other, 2 - 2 * links.core, at)
        down = set_at(down, down_half[:, None], at, links.core)
        down = set_at(down, down_other[:, None], at, 1 - links.core)
    return (
        up.reshape(4, links.shards * rows, features),
        down.reshape(4 * links.shards * rows, features),
    )


def other_x(links, block):
    sent = lax.dynamic_index_in_dim(block, 1 - links.x, 0, keepdims=False)
    kept = lax.dynamic_index_in_dim(block, links.x, 0, keepdims=False)
    return add_low(kept, links.swap(sent, "fsdp", 1))


def reduce_second(links, grad_up, grad_down):
    features = grad_down.shape[1]
    rows = features // links.shards
    up = grad_up.reshape(2, 2, links.depth, 2, rows, features)
    down = grad_down.reshape(links.depth, 2, 2, 2, rows, features)
    blocks = []
    for k in range(links.depth):
        at = links.block_at(k)
        up_k = lax.dynamic_index_in_dim(up, at, 2, keepdims=False).transpose(0, 2, 1, 3, 4)
        down_k = lax.dynamic_index_in_dim(down, at, 0, keepdims=False).transpose(1, 0, 2, 3, 4)
        both = jnp.stack([up_k, down_k])
        sent = lax.dynamic_index_in_dim(both, 1 - links.core, 1, keepdims=False)
        kept = lax.dynamic_index_in_dim(both, links.core, 1, keepdims=False)
        halves = add_low(kept, links.swap(sent, "context", 1))
        sent = jnp.where(links.even, halves[1], halves[0])
        kept = jnp.where(links.even, halves[0], halves[1])
        block = add_low(kept, links.swap(sent, "context", 2))
        block = links.sum_same_parity(block)
        blocks.append(other_x(links, block))
    mine = links.reduce_line(blocks).astype(jnp.bfloat16)
    other = links.swap(mine, "context", 2)
    up_half = jnp.where(links.even, mine, other)
    down_half = jnp.where(links.even, other, mine)
    both = jnp.stack([up_half, down_half])
    return join_cores(links, both)


def join_cores(links, half):
    other = links.swap(half, "context", 1)
    first = jnp.where(links.core == 0, half, other)
    last = jnp.where(links.core == 0, other, half)
    return jnp.concatenate([first, last], axis=-3).astype(jnp.float32)


def reduce_first(links, grads):
    features = grads.shape[1]
    rows = features // links.shards
    split = grads.reshape(2, 2, links.depth, 2, rows, features)
    blocks = []
    for k in range(links.depth):
        part = lax.dynamic_index_in_dim(split, links.block_at(k), 2, keepdims=False)
        part = part.transpose(0, 2, 1, 3, 4)
        sent = lax.dynamic_index_in_dim(part, 1 - links.core, 0, keepdims=False)
        kept = lax.dynamic_index_in_dim(part, links.core, 0, keepdims=False)
        blocks.append(other_x(links, add_low(kept, links.swap(sent, "context", 1))))
    mine = links.reduce_line(blocks).astype(jnp.bfloat16)
    mine = add_low(mine, links.swap(mine, "context", 2))
    mine = links.sum_same_parity(mine)
    return join_cores(links, mine)


def sum_everywhere(links, value):
    for axis, count in (("context", links.places), ("fsdp", links.shards)):
        bit = 1
        while bit < count:
            value = value + links.swap(value, axis, bit)
            bit *= 2
    return value


def dot_nt(left, right):
    return lax.dot_general(
        left, right, (((1,), (1,)), ((), ())), preferred_element_type=jnp.float32
    )


def dot_tn(left, right):
    return lax.dot_general(
        left, right, (((0,), (0,)), ((), ())), preferred_element_type=jnp.float32
    )


def lane_masks(pair, features, rows):
    lane = lax.broadcasted_iota(jnp.int32, (rows, 2 * HEAD_DIM), 1)
    inside = lane + pair * (2 * HEAD_DIM) < features
    return inside & (lane < HEAD_DIM), inside & (lane >= HEAD_DIM), inside


def allowed_pairs(key_segs, query_segs, diagonal):
    allowed = key_segs == query_segs
    if diagonal:
        shape = allowed.shape
        key_at = lax.broadcasted_iota(jnp.int32, shape, 0)
        query_at = lax.broadcasted_iota(jnp.int32, shape, 1)
        allowed = allowed & (key_at <= query_at)
    return allowed


def attend_kernel(features, place_ref, q_ref, k_ref, v_ref, kseg_ref, qseg_ref, o_ref, lse_ref):
    rows = q_ref.shape[0]
    masks = lane_masks(pl.program_id(1), features, rows)
    scaled = q_ref[...].astype(jnp.float32) * 0.125
    queries = [jnp.where(masks[h], scaled, 0.0).astype(jnp.bfloat16) for h in range(2)]
    query_segs = qseg_ref[...]

    def block(at, carry, diagonal):
        start = pl.multiple_of(at * rows, rows)
        keys = jnp.where(masks[2], k_ref[pl.ds(start, rows), :], 0.0).astype(jnp.bfloat16)
        values = jnp.where(masks[2], v_ref[pl.ds(start, rows), :], 0.0).astype(jnp.bfloat16)
        allowed = allowed_pairs(kseg_ref[pl.ds(start, rows), :], query_segs, diagonal)
        out = []
        for h in range(2):
            largest, total, mixed = carry[h]
            scores = jnp.where(allowed, dot_nt(keys, queries[h]), masked_score)
            newest = jnp.maximum(largest, jnp.max(scores, axis=0, keepdims=True))
            weights = jnp.exp(scores - newest)
            shrink = jnp.exp(largest - newest)
            total = total * shrink + jnp.sum(weights, axis=0, keepdims=True)
            mixed = mixed * shrink + dot_tn(values, weights.astype(jnp.bfloat16))
            out.append((newest, total, mixed))
        return tuple(out)

    first = (
        jnp.full((1, rows), masked_score, jnp.float32),
        jnp.zeros((1, rows), jnp.float32),
        jnp.zeros((2 * HEAD_DIM, rows), jnp.float32),
    )
    place = place_ref[0]
    carry = lax.fori_loop(0, place, lambda at, c: block(at, c, False), (first, first))
    carry = block(place, carry, True)
    parts = []
    for h in range(2):
        largest, total, mixed = carry[h]
        parts.append(mixed[h * HEAD_DIM : (h + 1) * HEAD_DIM] / total)
        lse_ref[h : h + 1, :] = largest + jnp.log(total)
    o_ref[...] = jnp.concatenate(parts, axis=0).T.astype(o_ref.dtype)


def attend_grads_kernel(
    features,
    place_ref,
    q_ref,
    k_ref,
    v_ref,
    g_ref,
    o_ref,
    lse_ref,
    kseg_ref,
    qseg_ref,
    dq_ref,
    dk_ref,
    dv_ref,
):
    rows = q_ref.shape[0]
    masks = lane_masks(pl.program_id(1), features, rows)
    scaled = q_ref[...].astype(jnp.float32) * 0.125
    grads = g_ref[...].astype(jnp.float32)
    queries = [jnp.where(masks[h], scaled, 0.0).astype(jnp.bfloat16) for h in range(2)]
    grad_heads = [jnp.where(masks[h], grads, 0.0).astype(jnp.bfloat16) for h in range(2)]
    products = jnp.where(masks[2], grads * o_ref[...].astype(jnp.float32), 0.0).T
    deltas = [
        jnp.sum(products[h * HEAD_DIM : (h + 1) * HEAD_DIM], axis=0, keepdims=True)
        for h in range(2)
    ]
    lses = [lse_ref[h : h + 1, :] for h in range(2)]
    query_segs = qseg_ref[...]

    def block(at, carry, diagonal):
        start = pl.multiple_of(at * rows, rows)
        keys = jnp.where(masks[2], k_ref[pl.ds(start, rows), :], 0.0).astype(jnp.bfloat16)
        values = jnp.where(masks[2], v_ref[pl.ds(start, rows), :], 0.0).astype(jnp.bfloat16)
        allowed = allowed_pairs(kseg_ref[pl.ds(start, rows), :], query_segs, diagonal)
        out, grad_keys, grad_values = [], 0.0, 0.0
        for h in range(2):
            scores = jnp.where(allowed, dot_nt(keys, queries[h]), masked_score)
            probs = jnp.exp(scores - lses[h])
            grad_scores = probs * (dot_nt(values, grad_heads[h]) - deltas[h])
            grad_scores = grad_scores.astype(jnp.bfloat16)
            out.append(carry[h] + dot_tn(keys, grad_scores))
            grad_keys += jnp.dot(grad_scores, queries[h], preferred_element_type=jnp.float32)
            grad_values += jnp.dot(
                probs.astype(jnp.bfloat16), grad_heads[h], preferred_element_type=jnp.float32
            )
        dk_ref[pl.ds(start, rows), :] = grad_keys.astype(dk_ref.dtype)
        dv_ref[pl.ds(start, rows), :] = grad_values.astype(dv_ref.dtype)
        return tuple(out)

    place = place_ref[0]
    blank = jnp.zeros((2 * HEAD_DIM, rows), jnp.float32)
    carry = lax.fori_loop(0, place, lambda at, c: block(at, c, False), (blank, blank))
    carry = block(place, carry, True)

    def clear(at, _):
        start = pl.multiple_of(at * rows, rows)
        dk_ref[pl.ds(start, rows), :] = jnp.zeros((rows, 2 * HEAD_DIM), dk_ref.dtype)
        dv_ref[pl.ds(start, rows), :] = jnp.zeros((rows, 2 * HEAD_DIM), dv_ref.dtype)
        return 0

    lax.fori_loop(place + 1, k_ref.shape[0] // rows, clear, 0)
    both = [carry[h][h * HEAD_DIM : (h + 1) * HEAD_DIM] for h in range(2)]
    dq_ref[...] = (jnp.concatenate(both, axis=0).T * 0.125).astype(dq_ref.dtype)


def attention_specs(sequences, stretch, length, features):
    wide = 2 * HEAD_DIM
    pairs = -(-features // wide)
    own = pl.BlockSpec((None, stretch, wide), lambda s, p: (s, 0, p))
    whole = pl.BlockSpec((None, length, wide), lambda s, p: (s, 0, p))
    lse = pl.BlockSpec((None, None, 2, stretch), lambda s, p: (s, p, 0, 0))
    key_segs = pl.BlockSpec((None, length, 1), lambda s, p: (s, 0, 0))
    query_segs = pl.BlockSpec((None, 1, stretch), lambda s, p: (s, 0, 0))
    place = pl.BlockSpec(memory_space=pltpu.SMEM)
    return pairs, own, whole, lse, key_segs, query_segs, place


def attend(place, queries, keys, values, key_segs, query_segs):
    sequences, stretch, features = queries.shape
    length = keys.shape[1]
    pairs, own, whole, lse, kseg, qseg, at = attention_specs(sequences, stretch, length, features)
    return pl.pallas_call(
        functools.partial(attend_kernel, features),
        grid=(sequences, pairs),
        in_specs=[at, own, whole, whole, kseg, qseg],
        out_specs=[own, lse],
        out_shape=[
            jax.ShapeDtypeStruct(queries.shape, jnp.bfloat16),
            jax.ShapeDtypeStruct((sequences, pairs, 2, stretch), jnp.float32),
        ],
        compiler_params=pltpu.CompilerParams(vmem_limit_bytes=40 * 2**20),
        cost_estimate=pl.CostEstimate(
            flops=16 * pairs * sequences * stretch * length * HEAD_DIM,
            bytes_accessed=8 * queries.size + 4 * keys.size,
            transcendentals=0,
        ),
    )(place, queries, keys, values, key_segs, query_segs)


def attend_grads(place, queries, keys, values, grads, attended, lse_rows, key_segs, query_segs):
    sequences, stretch, features = queries.shape
    length = keys.shape[1]
    pairs, own, whole, lse, kseg, qseg, at = attention_specs(sequences, stretch, length, features)
    return pl.pallas_call(
        functools.partial(attend_grads_kernel, features),
        grid=(sequences, pairs),
        in_specs=[at, own, whole, whole, own, own, lse, kseg, qseg],
        out_specs=[own, whole, whole],
        out_shape=[
            jax.ShapeDtypeStruct(queries.shape, jnp.bfloat16),
            jax.ShapeDtypeStruct(keys.shape, jnp.bfloat16),
            jax.ShapeDtypeStruct(keys.shape, jnp.bfloat16),
        ],
        compiler_params=pltpu.CompilerParams(vmem_limit_bytes=40 * 2**20),
        cost_estimate=pl.CostEstimate(
            flops=40 * pairs * sequences * stretch * length * HEAD_DIM,
            bytes_accessed=8 * queries.size + 8 * keys.size,
            transcendentals=0,
        ),
    )(place, queries, keys, values, grads, attended, lse_rows, key_segs, query_segs)


def gather_small(links, vector):
    full = jnp.zeros((links.shards, vector.shape[0]), vector.dtype)
    for k, pair in enumerate(links.gather_pairs(vector)):
        full = set_at(full, pair, 2 * links.block_at(k))
    return full


def gather_stretches(links, mine):
    have = mine[:, None]
    bit = links.places // 2
    while bit >= 1:
        pairs = [(i, i ^ bit) for i in range(links.places)]
        if bit == links.places // 2:
            pairs = [(i, j) for i, j in pairs if i < j]
        other = lax.ppermute(have, "context", pairs)
        lower = (links.place // bit) % 2 == 0
        first, last = jnp.where(lower, have, other), jnp.where(lower, other, have)
        have = jnp.stack([first, last], axis=2)
        have = have.reshape(have.shape[0], -1, *have.shape[3:])
        bit //= 2
    return have


def reduce_stretches(links, parts):
    bit = 1
    while bit < links.places:
        split = parts.reshape(-1, 2, *parts.shape[1:])
        digit = (links.place // bit) % 2
        sent = lax.dynamic_index_in_dim(split, 1 - digit, 1, keepdims=False)
        kept = lax.dynamic_index_in_dim(split, digit, 1, keepdims=False)
        pairs = [(i, i ^ bit) for i in range(links.places)]
        if bit == links.places // 2:
            pairs = [(i, j) for i, j in pairs if i > j]
        parts = add_low(kept, lax.ppermute(sent, "context", pairs))
        bit *= 2
    return parts[0]


def local(
    block_input,
    segment_ids,
    ln1_gain,
    ln1_bias,
    w_qkv,
    bias_query,
    bias_value,
    w_out,
    bias_out,
    ln2_gain,
    ln2_bias,
    w_up,
    bias_up,
    w_down,
    bias_down,
    cotangent,
):
    sequences, stretch, features = block_input.shape
    head_count = features // HEAD_DIM
    length_all = stretch * lax.axis_size("context")
    offset = lax.axis_index("context") * stretch
    tokens = sequences * stretch
    links = Links()
    small = (
        ln1_gain, ln1_bias, bias_query, bias_value, bias_out, ln2_gain, ln2_bias, bias_down, bias_up
    )
    small_all = gather_small(links, jnp.concatenate(small))
    small_full, start = [], 0
    for vector in small:
        small_full.append(small_all[:, start : start + vector.shape[0]].reshape(-1))
        start += vector.shape[0]
    (
        gain_one,
        shift_one,
        query_bias,
        value_bias,
        out_bias,
        gain_two,
        shift_two,
        down_bias,
        up_bias,
    ) = small_full
    full_first = gather_first(links, w_qkv, w_out)
    full_up, full_down = gather_second(links, w_up, w_down)
    full_out = full_first[3]
    gain_one = gain_one.astype(jnp.float32)
    shift_one = shift_one.astype(jnp.float32)
    gain_two = gain_two.astype(jnp.float32)
    shift_two = shift_two.astype(jnp.float32)
    inputs = block_input.reshape(tokens, features).astype(jnp.float32)
    normed = normalize(inputs, gain_one, shift_one).astype(jnp.bfloat16)
    inputs_all = gather_stretches(links, block_input).reshape(-1, features)
    normed_all = normalize(inputs_all.astype(jnp.float32), gain_one, shift_one)
    normed_all = normed_all.astype(jnp.bfloat16)
    queries = jnp.dot(normed, full_first[0], preferred_element_type=jnp.float32)
    keys_all = jnp.dot(normed_all, full_first[1], preferred_element_type=jnp.float32)
    values_all = jnp.dot(normed_all, full_first[2], preferred_element_type=jnp.float32)
    queries = (queries + query_bias.astype(jnp.float32)).astype(jnp.bfloat16)
    keys_all = keys_all.astype(jnp.bfloat16).reshape(sequences, length_all, features)
    values_all = values_all + value_bias.astype(jnp.float32)
    values_all = values_all.astype(jnp.bfloat16).reshape(sequences, length_all, features)
    query_seqs = queries.reshape(sequences, stretch, features)
    own_segs = lax.dynamic_slice_in_dim(segment_ids, offset, stretch, 1)[:, None, :]
    key_segs = segment_ids[:, :, None]
    place = links.place.astype(jnp.int32).reshape(1)
    attended_seqs, lse_kept = attend(
        place, query_seqs, keys_all, values_all, key_segs, own_segs
    )
    attended = attended_seqs.reshape(tokens, features)
    middle = (
        inputs
        + jnp.dot(attended, full_out, preferred_element_type=jnp.float32)
        + out_bias.astype(jnp.float32)
    )
    normed_two = normalize(middle, gain_two, shift_two).astype(jnp.bfloat16)
    pre_act = jnp.concatenate(
        [jnp.dot(normed_two, full_up[j], preferred_element_type=jnp.float32) for j in range(4)],
        axis=1,
    ) + up_bias.astype(jnp.float32)
    hidden = gelu_tanh(pre_act).astype(jnp.bfloat16)
    result = (
        middle
        + jnp.dot(hidden, full_down, preferred_element_type=jnp.float32)
        + down_bias.astype(jnp.float32)
    )
    block_output = result.astype(jnp.bfloat16).reshape(block_input.shape)
    grad_out = cotangent.reshape(tokens, features)
    grad_out_f = grad_out.astype(jnp.float32)
    grad_w_down = contract_rows(hidden, grad_out).astype(jnp.bfloat16)
    grad_b_down = jnp.sum(grad_out_f, axis=0)
    grad_hidden = contract_cols(grad_out, full_down)
    gelu_value, gelu_pull = jax.vjp(gelu_tanh, pre_act)
    grad_pre = gelu_pull(grad_hidden)[0].astype(jnp.bfloat16)
    grad_w_up = jnp.stack(
        [
            contract_rows(normed_two, grad_pre[:, j * features : (j + 1) * features])
            for j in range(4)
        ]
    ).astype(jnp.bfloat16)
    second_sums = reduce_second(links, grad_w_up, grad_w_down)
    grad_b_up = jnp.sum(grad_pre.astype(jnp.float32), axis=0)
    grad_normed_two = sum(
        contract_cols(grad_pre[:, j * features : (j + 1) * features], full_up[j]) for j in range(4)
    )
    norm_value, norm_pull = jax.vjp(normalize, middle, gain_two, shift_two)
    grad_middle_part, grad_gain_two, grad_shift_two = norm_pull(grad_normed_two)
    grad_middle = grad_out_f + grad_middle_part
    grad_middle_low = grad_middle.astype(jnp.bfloat16)
    grad_w_out = contract_rows(attended, grad_middle_low)
    grad_b_out = jnp.sum(grad_middle_low.astype(jnp.float32), axis=0)
    grad_attended = contract_cols(grad_middle_low, full_out).astype(jnp.bfloat16)
    grad_att_seqs = grad_attended.reshape(sequences, stretch, features)

    grad_queries, key_parts, value_parts = attend_grads(
        place,
        query_seqs,
        keys_all,
        values_all,
        grad_att_seqs,
        attended_seqs,
        lse_kept,
        key_segs,
        own_segs,
    )
    grad_queries = grad_queries.reshape(tokens, features)
    key_rows = key_parts.reshape(-1, features)
    value_rows = value_parts.reshape(-1, features)
    parts = jnp.stack([key_parts, value_parts])
    parts = parts.reshape(2, sequences, links.places, stretch, features).transpose(2, 0, 1, 3, 4)
    own_parts = reduce_stretches(links, parts)
    grad_keys = own_parts[0].reshape(tokens, features)
    grad_values = own_parts[1].reshape(tokens, features)
    grads_first = jnp.stack(
        [
            contract_rows(normed, grad_queries),
            contract_rows(normed_all, key_rows),
            contract_rows(normed_all, value_rows),
            grad_w_out,
        ]
    ).astype(jnp.bfloat16)
    first_sums = reduce_first(links, grads_first)
    grad_b_query = jnp.sum(grad_queries.astype(jnp.float32), axis=0)
    grad_b_value = jnp.sum(value_rows.astype(jnp.float32), axis=0)
    grad_normed = (
        contract_cols(grad_queries, full_first[0])
        + contract_cols(grad_keys, full_first[1])
        + contract_cols(grad_values, full_first[2])
    )
    first_value, first_pull = jax.vjp(normalize, inputs, gain_one, shift_one)
    grad_input_part, grad_gain_one, grad_shift_one = first_pull(grad_normed)
    input_grad = (grad_middle + grad_input_part).reshape(block_input.shape)
    vectors = (
        grad_gain_one,
        grad_shift_one,
        grad_b_query,
        grad_b_value,
        grad_b_out,
        grad_gain_two,
        grad_shift_two,
        grad_b_down,
        grad_b_up,
    )
    vector_sums = sum_everywhere(links, jnp.concatenate(vectors))
    mine, start = [], 0
    for vector in vectors:
        size = vector.shape[0]
        own = size // links.shards
        mine.append(lax.dynamic_slice_in_dim(vector_sums, start + links.shard * own, own, 0))
        start += size
    up_sum, down_sum = second_sums[0], second_sums[1]
    return (
        block_output,
        input_grad,
        mine[0],
        mine[1],
        jnp.concatenate([first_sums[j] for j in range(3)], axis=1),
        mine[2],
        mine[3],
        first_sums[3],
        mine[4],
        mine[5],
        mine[6],
        jnp.concatenate([up_sum[j] for j in range(4)], axis=1),
        mine[8],
        down_sum.reshape(-1, features),
        mine[7],
    )


def solution(mesh):
    in_specs = (
        P("fsdp", "context", None),
        P("fsdp", None),
        P("fsdp"),
        P("fsdp"),
        P("fsdp", None),
        P("fsdp"),
        P("fsdp"),
        P("fsdp", None),
        P("fsdp"),
        P("fsdp"),
        P("fsdp"),
        P("fsdp", None),
        P("fsdp"),
        P("fsdp", None),
        P("fsdp"),
        P("fsdp", "context", None),
    )
    out_specs = (
        P("fsdp", "context", None),
        P("fsdp", "context", None),
        P("fsdp"),
        P("fsdp"),
        P("fsdp", None),
        P("fsdp"),
        P("fsdp"),
        P("fsdp", None),
        P("fsdp"),
        P("fsdp"),
        P("fsdp"),
        P("fsdp", None),
        P("fsdp"),
        P("fsdp", None),
        P("fsdp"),
    )
    return jax.shard_map(local, mesh=mesh, in_specs=in_specs, out_specs=out_specs, check_vma=False)
```

```python
import functools

import jax
import jax.numpy as jnp
from jax import lax
from jax.experimental import pallas as pl
from jax.experimental.pallas import tpu as pltpu
from jax.sharding import PartitionSpec as P

HEAD_DIM = 64


masked_score = -1e30


def normalize(inputs, scale_vec, shift_vec):
    average = jnp.mean(inputs, axis=-1, keepdims=True)
    centered = inputs - average
    variance = jnp.mean(centered * centered, axis=-1, keepdims=True)
    return centered * lax.rsqrt(variance + 1e-05) * scale_vec + shift_vec


def gelu_tanh(pre_act):
    return jax.nn.gelu(pre_act, approximate=True)


def contract_rows(left, right):
    return lax.dot_general(
        left, right, (((0,), (0,)), ((), ())), preferred_element_type=jnp.float32
    )


def contract_cols(left, right):
    return lax.dot_general(
        left, right, (((1,), (1,)), ((), ())), preferred_element_type=jnp.float32
    )

class Links:
    def __init__(self):
        self.shards = lax.axis_size("fsdp")
        self.places = lax.axis_size("context")
        self.depth = self.shards // 2
        self.shard = lax.axis_index("fsdp")
        self.place = lax.axis_index("context")
        self.z = self.shard // 2
        self.x = self.shard % 2
        self.core = self.place % 2
        self.even = (self.place // 2) % 2 == 0

    def swap(self, value, axis, bit):
        count = lax.axis_size(axis)
        return lax.ppermute(value, axis, [(i, i ^ bit) for i in range(count)])

    def right(self, value, distance):
        pairs = []
        for z in range(self.depth - 1):
            if z + 1 >= distance:
                pairs += [(2 * z, 2 * z + 2), (2 * z + 1, 2 * z + 3)]
        return lax.ppermute(value, "fsdp", pairs)

    def left(self, value, distance):
        pairs = []
        for z in range(1, self.depth):
            if z - 1 + distance < self.depth:
                pairs += [(2 * z, 2 * z - 2), (2 * z + 1, 2 * z - 1)]
        return lax.ppermute(value, "fsdp", pairs)

    def block_at(self, k):
        return lax.rem(self.z + k, self.depth)

    def gather_pairs(self, mine):
        rights, lefts = [mine], [mine]
        for distance in range(1, self.depth):
            rights.append(self.right(rights[-1], distance))
            lefts.append(self.left(lefts[-1], distance))
        pairs = []
        for k in range(self.depth):
            if k == 0:
                block = mine
            else:
                block = jnp.where(self.z + k < self.depth, lefts[k], rights[self.depth - k])
            other = self.swap(block, "fsdp", 1)
            pairs.append(
                jnp.stack(
                    [jnp.where(self.x == 0, block, other), jnp.where(self.x == 0, other, block)]
                )
            )
        return pairs

    def reduce_line(self, blocks):
        from_left, from_right = None, None
        for distance in range(self.depth - 1, 0, -1):
            going_right = blocks[distance].astype(jnp.float32)
            going_left = blocks[self.depth - distance].astype(jnp.float32)
            if from_left is not None:
                going_right = going_right + from_left.astype(jnp.float32)
                going_left = going_left + from_right.astype(jnp.float32)
            right_pairs, left_pairs = [], []
            for z in range(self.depth - distance):
                right_pairs += [(2 * z, 2 * z + 2), (2 * z + 1, 2 * z + 3)]
            for z in range(distance, self.depth):
                left_pairs += [(2 * z, 2 * z - 2), (2 * z + 1, 2 * z - 1)]
            from_left = lax.ppermute(going_right.astype(jnp.bfloat16), "fsdp", right_pairs)
            from_right = lax.ppermute(going_left.astype(jnp.bfloat16), "fsdp", left_pairs)
        total = blocks[0].astype(jnp.float32)
        if from_left is not None:
            total = total + from_left.astype(jnp.float32) + from_right.astype(jnp.float32)
        return total

    def sum_same_parity(self, value):
        bit = 4
        while bit < self.places:
            value = add_low(value, self.swap(value, "context", bit))
            bit *= 2
        return value


def add_low(left, right):
    return (left.astype(jnp.float32) + right.astype(jnp.float32)).astype(jnp.bfloat16)


def set_at(buffer, block, *at):
    at = at + (0,) * (buffer.ndim - len(at))
    return lax.dynamic_update_slice(buffer, block, tuple(jnp.asarray(i, jnp.int32) for i in at))


def quarters(shard, features):
    return jnp.stack([shard[:, j * features : (j + 1) * features] for j in range(4)])


def gather_first(links, w_qkv, w_out):
    rows, features = w_out.shape
    own = quarters(jnp.concatenate([w_qkv, w_out], axis=1), features)
    mine = lax.dynamic_slice_in_dim(own, 2 * links.core, 2, 0)
    full = jnp.zeros((4, links.shards, rows, features), jnp.bfloat16)
    for k, pair in enumerate(links.gather_pairs(mine)):
        block = pair.transpose(1, 0, 2, 3)
        other = links.swap(block, "context", 1)
        at = 2 * links.block_at(k)
        full = set_at(full, block, 2 * links.core, at)
        full = set_at(full, other, 2 - 2 * links.core, at)
    return full.reshape(4, links.shards * rows, features)


def begin_second(links, w_up, w_down):
    rows = w_up.shape[0]
    features = w_down.shape[1]
    own_up = lax.dynamic_slice_in_dim(quarters(w_up, features), 2 * links.core, 2, 0)
    own_down = lax.dynamic_index_in_dim(
        w_down.reshape(2, 2, rows, features), links.core, 0, keepdims=False
    )
    mine = jnp.where(links.even, own_up, own_down)
    pairs = links.gather_pairs(mine)
    return pairs, [links.swap(pair, "context", 2) for pair in pairs]


def finish_second(links, pairs, others):
    rows, features = pairs[0].shape[-2:]
    up = jnp.zeros((4, links.shards, rows, features), jnp.bfloat16)
    down = jnp.zeros((links.shards, 2, 2, rows, features), jnp.bfloat16)
    for k, (pair, other) in enumerate(zip(pairs, others)):
        up_half = jnp.where(links.even, pair, other).transpose(1, 0, 2, 3)
        down_half = jnp.where(links.even, other, pair)
        up_other = links.swap(up_half, "context", 1)
        down_other = links.swap(down_half, "context", 1)
        at = 2 * links.block_at(k)
        up = set_at(up, up_half, 2 * links.core, at)
        up = set_at(up, up_other, 2 - 2 * links.core, at)
        down = set_at(down, down_half[:, None], at, links.core)
        down = set_at(down, down_other[:, None], at, 1 - links.core)
    return (
        up.reshape(4, links.shards * rows, features),
        down.reshape(4 * links.shards * rows, features),
    )


def other_x(links, block):
    sent = lax.dynamic_index_in_dim(block, 1 - links.x, 0, keepdims=False)
    kept = lax.dynamic_index_in_dim(block, links.x, 0, keepdims=False)
    return add_low(kept, links.swap(sent, "fsdp", 1))


def core_halves(links, grads):
    halves = []
    for j in range(2):
        kept = jnp.where(links.core == 0, grads[j], grads[2 + j])
        sent = jnp.where(links.core == 0, grads[2 + j], grads[j])
        halves.append(add_low(kept, links.swap(sent, "context", 1)))
    return halves


def core_rows(links, grad_down):
    features = grad_down.shape[1]
    split = grad_down.reshape(links.depth, 2, 2, 2, features // links.shards, features)
    sent = lax.dynamic_index_in_dim(split, 1 - links.core, 2, keepdims=False)
    kept = lax.dynamic_index_in_dim(split, links.core, 2, keepdims=False)
    return add_low(kept, links.swap(sent, "context", 1))


def block_of(links, halves, at):
    features = halves[0].shape[1]
    parts = [
        half.reshape(links.depth, 2, features // links.shards, features) for half in halves
    ]
    return jnp.stack(
        [lax.dynamic_index_in_dim(part, at, 0, keepdims=False) for part in parts], axis=1
    )


def reduce_second(links, up_halves, down_half):
    blocks = []
    for k in range(links.depth):
        at = links.block_at(k)
        up_k = block_of(links, up_halves, at)
        down_k = lax.dynamic_index_in_dim(down_half, at, 0, keepdims=False)
        sent = jnp.where(links.even, down_k, up_k)
        kept = jnp.where(links.even, up_k, down_k)
        block = add_low(kept, links.swap(sent, "context", 2))
        block = links.sum_same_parity(block)
        blocks.append(other_x(links, block))
    mine = links.reduce_line(blocks).astype(jnp.bfloat16)
    other = links.swap(mine, "context", 2)
    up_half = jnp.where(links.even, mine, other)
    down_half = jnp.where(links.even, other, mine)
    both = jnp.stack([up_half, down_half])
    return join_cores(links, both)


def join_cores(links, half):
    other = links.swap(half, "context", 1)
    first = jnp.where(links.core == 0, half, other)
    last = jnp.where(links.core == 0, other, half)
    return jnp.concatenate([first, last], axis=-3).astype(jnp.float32)


def reduce_first(links, grads):
    halves = core_halves(links, grads)
    blocks = [
        other_x(links, block_of(links, halves, links.block_at(k))) for k in range(links.depth)
    ]
    mine = links.reduce_line(blocks).astype(jnp.bfloat16)
    mine = add_low(mine, links.swap(mine, "context", 2))
    mine = links.sum_same_parity(mine)
    return join_cores(links, mine)


def sum_everywhere(links, value):
    for axis, count in (("context", links.places), ("fsdp", links.shards)):
        bit = 1
        while bit < count:
            value = value + links.swap(value, axis, bit)
            bit *= 2
    return value


def dot_nt(left, right):
    return lax.dot_general(
        left, right, (((1,), (1,)), ((), ())), preferred_element_type=jnp.float32
    )


def dot_tn(left, right):
    return lax.dot_general(
        left, right, (((0,), (0,)), ((), ())), preferred_element_type=jnp.float32
    )


def lane_masks(pair, features, rows):
    lane = lax.broadcasted_iota(jnp.int32, (rows, 2 * HEAD_DIM), 1)
    inside = lane + pair * (2 * HEAD_DIM) < features
    return inside & (lane < HEAD_DIM), inside & (lane >= HEAD_DIM), inside


def allowed_pairs(key_segs, query_segs, diagonal):
    allowed = key_segs == query_segs
    if diagonal:
        shape = allowed.shape
        key_at = lax.broadcasted_iota(jnp.int32, shape, 0)
        query_at = lax.broadcasted_iota(jnp.int32, shape, 1)
        allowed = allowed & (key_at <= query_at)
    return allowed


def attend_kernel(features, place_ref, q_ref, k_ref, v_ref, kseg_ref, qseg_ref, o_ref, lse_ref):
    rows = q_ref.shape[0]
    masks = lane_masks(pl.program_id(1), features, rows)
    scaled = q_ref[...].astype(jnp.float32) * 0.125
    queries = [jnp.where(masks[h], scaled, 0.0).astype(jnp.bfloat16) for h in range(2)]
    query_segs = qseg_ref[...]

    def block(at, carry, diagonal):
        start = pl.multiple_of(at * rows, rows)
        keys = jnp.where(masks[2], k_ref[pl.ds(start, rows), :], 0.0).astype(jnp.bfloat16)
        values = jnp.where(masks[2], v_ref[pl.ds(start, rows), :], 0.0).astype(jnp.bfloat16)
        allowed = allowed_pairs(kseg_ref[pl.ds(start, rows), :], query_segs, diagonal)
        out = []
        for h in range(2):
            largest, total, mixed = carry[h]
            scores = jnp.where(allowed, dot_nt(keys, queries[h]), masked_score)
            newest = jnp.maximum(largest, jnp.max(scores, axis=0, keepdims=True))
            weights = jnp.exp(scores - newest)
            shrink = jnp.exp(largest - newest)
            total = total * shrink + jnp.sum(weights, axis=0, keepdims=True)
            mixed = mixed * shrink + dot_tn(values, weights.astype(jnp.bfloat16))
            out.append((newest, total, mixed))
        return tuple(out)

    first = (
        jnp.full((1, rows), masked_score, jnp.float32),
        jnp.zeros((1, rows), jnp.float32),
        jnp.zeros((2 * HEAD_DIM, rows), jnp.float32),
    )
    place = place_ref[0]
    carry = lax.fori_loop(0, place, lambda at, c: block(at, c, False), (first, first))
    carry = block(place, carry, True)
    parts = []
    for h in range(2):
        largest, total, mixed = carry[h]
        parts.append(mixed[h * HEAD_DIM : (h + 1) * HEAD_DIM] / total)
        lse_ref[h : h + 1, :] = largest + jnp.log(total)
    o_ref[...] = jnp.concatenate(parts, axis=0).T.astype(o_ref.dtype)


def attend_grads_kernel(
    features,
    place_ref,
    q_ref,
    k_ref,
    v_ref,
    g_ref,
    o_ref,
    lse_ref,
    kseg_ref,
    qseg_ref,
    dq_ref,
    dk_ref,
    dv_ref,
):
    rows = q_ref.shape[0]
    masks = lane_masks(pl.program_id(1), features, rows)
    scaled = q_ref[...].astype(jnp.float32) * 0.125
    grads = g_ref[...].astype(jnp.float32)
    queries = [jnp.where(masks[h], scaled, 0.0).astype(jnp.bfloat16) for h in range(2)]
    grad_heads = [jnp.where(masks[h], grads, 0.0).astype(jnp.bfloat16) for h in range(2)]
    products = jnp.where(masks[2], grads * o_ref[...].astype(jnp.float32), 0.0).T
    deltas = [
        jnp.sum(products[h * HEAD_DIM : (h + 1) * HEAD_DIM], axis=0, keepdims=True)
        for h in range(2)
    ]
    lses = [lse_ref[h : h + 1, :] for h in range(2)]
    query_segs = qseg_ref[...]

    def block(at, carry, diagonal):
        start = pl.multiple_of(at * rows, rows)
        keys = jnp.where(masks[2], k_ref[pl.ds(start, rows), :], 0.0).astype(jnp.bfloat16)
        values = jnp.where(masks[2], v_ref[pl.ds(start, rows), :], 0.0).astype(jnp.bfloat16)
        allowed = allowed_pairs(kseg_ref[pl.ds(start, rows), :], query_segs, diagonal)
        out, grad_keys, grad_values = [], 0.0, 0.0
        for h in range(2):
            scores = jnp.where(allowed, dot_nt(keys, queries[h]), masked_score)
            probs = jnp.exp(scores - lses[h])
            grad_scores = probs * (dot_nt(values, grad_heads[h]) - deltas[h])
            grad_scores = grad_scores.astype(jnp.bfloat16)
            out.append(carry[h] + dot_tn(keys, grad_scores))
            grad_keys += jnp.dot(grad_scores, queries[h], preferred_element_type=jnp.float32)
            grad_values += jnp.dot(
                probs.astype(jnp.bfloat16), grad_heads[h], preferred_element_type=jnp.float32
            )
        dk_ref[pl.ds(start, rows), :] = grad_keys.astype(dk_ref.dtype)
        dv_ref[pl.ds(start, rows), :] = grad_values.astype(dv_ref.dtype)
        return tuple(out)

    place = place_ref[0]
    blank = jnp.zeros((2 * HEAD_DIM, rows), jnp.float32)
    carry = lax.fori_loop(0, place, lambda at, c: block(at, c, False), (blank, blank))
    carry = block(place, carry, True)

    def clear(at, _):
        start = pl.multiple_of(at * rows, rows)
        dk_ref[pl.ds(start, rows), :] = jnp.zeros((rows, 2 * HEAD_DIM), dk_ref.dtype)
        dv_ref[pl.ds(start, rows), :] = jnp.zeros((rows, 2 * HEAD_DIM), dv_ref.dtype)
        return 0

    lax.fori_loop(place + 1, k_ref.shape[0] // rows, clear, 0)
    both = [carry[h][h * HEAD_DIM : (h + 1) * HEAD_DIM] for h in range(2)]
    dq_ref[...] = (jnp.concatenate(both, axis=0).T * 0.125).astype(dq_ref.dtype)


def attention_specs(sequences, stretch, length, features):
    wide = 2 * HEAD_DIM
    pairs = -(-features // wide)
    own = pl.BlockSpec((None, stretch, wide), lambda s, p: (s, 0, p))
    whole = pl.BlockSpec((None, length, wide), lambda s, p: (s, 0, p))
    lse = pl.BlockSpec((None, None, 2, stretch), lambda s, p: (s, p, 0, 0))
    key_segs = pl.BlockSpec((None, length, 1), lambda s, p: (s, 0, 0))
    query_segs = pl.BlockSpec((None, 1, stretch), lambda s, p: (s, 0, 0))
    place = pl.BlockSpec(memory_space=pltpu.SMEM)
    return pairs, own, whole, lse, key_segs, query_segs, place


def attend(place, queries, keys, values, key_segs, query_segs):
    sequences, stretch, features = queries.shape
    length = keys.shape[1]
    pairs, own, whole, lse, kseg, qseg, at = attention_specs(sequences, stretch, length, features)
    return pl.pallas_call(
        functools.partial(attend_kernel, features),
        grid=(sequences, pairs),
        in_specs=[at, own, whole, whole, kseg, qseg],
        out_specs=[own, lse],
        out_shape=[
            jax.ShapeDtypeStruct(queries.shape, jnp.bfloat16),
            jax.ShapeDtypeStruct((sequences, pairs, 2, stretch), jnp.float32),
        ],
        compiler_params=pltpu.CompilerParams(vmem_limit_bytes=40 * 2**20),
        cost_estimate=pl.CostEstimate(
            flops=16 * pairs * sequences * stretch * length * HEAD_DIM,
            bytes_accessed=8 * queries.size + 4 * keys.size,
            transcendentals=0,
        ),
    )(place, queries, keys, values, key_segs, query_segs)


def attend_grads(place, queries, keys, values, grads, attended, lse_rows, key_segs, query_segs):
    sequences, stretch, features = queries.shape
    length = keys.shape[1]
    pairs, own, whole, lse, kseg, qseg, at = attention_specs(sequences, stretch, length, features)
    return pl.pallas_call(
        functools.partial(attend_grads_kernel, features),
        grid=(sequences, pairs),
        in_specs=[at, own, whole, whole, own, own, lse, kseg, qseg],
        out_specs=[own, whole, whole],
        out_shape=[
            jax.ShapeDtypeStruct(queries.shape, jnp.bfloat16),
            jax.ShapeDtypeStruct(keys.shape, jnp.bfloat16),
            jax.ShapeDtypeStruct(keys.shape, jnp.bfloat16),
        ],
        compiler_params=pltpu.CompilerParams(vmem_limit_bytes=40 * 2**20),
        cost_estimate=pl.CostEstimate(
            flops=40 * pairs * sequences * stretch * length * HEAD_DIM,
            bytes_accessed=8 * queries.size + 8 * keys.size,
            transcendentals=0,
        ),
    )(place, queries, keys, values, grads, attended, lse_rows, key_segs, query_segs)


def gather_small(links, vector):
    full = jnp.zeros((links.shards, vector.shape[0]), vector.dtype)
    for k, pair in enumerate(links.gather_pairs(vector)):
        full = set_at(full, pair, 2 * links.block_at(k))
    return full


def gather_stretches(links, mine):
    have = mine[:, None]
    bit = links.places // 2
    while bit >= 1:
        pairs = [(i, i ^ bit) for i in range(links.places)]
        if bit == links.places // 2:
            pairs = [(i, j) for i, j in pairs if i < j]
        other = lax.ppermute(have, "context", pairs)
        lower = (links.place // bit) % 2 == 0
        first, last = jnp.where(lower, have, other), jnp.where(lower, other, have)
        have = jnp.stack([first, last], axis=2)
        have = have.reshape(have.shape[0], -1, *have.shape[3:])
        bit //= 2
    return have


def reduce_stretches(links, parts):
    bit = 1
    while bit < links.places:
        split = parts.reshape(-1, 2, *parts.shape[1:])
        digit = (links.place // bit) % 2
        sent = lax.dynamic_index_in_dim(split, 1 - digit, 1, keepdims=False)
        kept = lax.dynamic_index_in_dim(split, digit, 1, keepdims=False)
        pairs = [(i, i ^ bit) for i in range(links.places)]
        if bit == links.places // 2:
            pairs = [(i, j) for i, j in pairs if i > j]
        parts = add_low(kept, lax.ppermute(sent, "context", pairs))
        bit *= 2
    return parts[0]


def local(
    block_input,
    segment_ids,
    ln1_gain,
    ln1_bias,
    w_qkv,
    bias_query,
    bias_value,
    w_out,
    bias_out,
    ln2_gain,
    ln2_bias,
    w_up,
    bias_up,
    w_down,
    bias_down,
    cotangent,
):
    sequences, stretch, features = block_input.shape
    head_count = features // HEAD_DIM
    length_all = stretch * lax.axis_size("context")
    offset = lax.axis_index("context") * stretch
    tokens = sequences * stretch
    links = Links()
    small = (
        ln1_gain, ln1_bias, bias_query, bias_value, bias_out, ln2_gain, ln2_bias, bias_down, bias_up
    )
    small_all = gather_small(links, jnp.concatenate(small))
    small_full, start = [], 0
    for vector in small:
        small_full.append(small_all[:, start : start + vector.shape[0]].reshape(-1))
        start += vector.shape[0]
    (
        gain_one,
        shift_one,
        query_bias,
        value_bias,
        out_bias,
        gain_two,
        shift_two,
        down_bias,
        up_bias,
    ) = small_full
    full_first = gather_first(links, w_qkv, w_out)
    second_pairs, second_others = begin_second(links, w_up, w_down)
    full_out = full_first[3]
    gain_one = gain_one.astype(jnp.float32)
    shift_one = shift_one.astype(jnp.float32)
    gain_two = gain_two.astype(jnp.float32)
    shift_two = shift_two.astype(jnp.float32)
    inputs = block_input.reshape(tokens, features).astype(jnp.float32)
    normed = normalize(inputs, gain_one, shift_one).astype(jnp.bfloat16)
    inputs_all = gather_stretches(links, block_input).reshape(-1, features)
    normed_all = normalize(inputs_all.astype(jnp.float32), gain_one, shift_one)
    normed_all = normed_all.astype(jnp.bfloat16)
    queries = jnp.dot(normed, full_first[0], preferred_element_type=jnp.float32)
    keys_all = jnp.dot(normed_all, full_first[1], preferred_element_type=jnp.float32)
    values_all = jnp.dot(normed_all, full_first[2], preferred_element_type=jnp.float32)
    queries = (queries + query_bias.astype(jnp.float32)).astype(jnp.bfloat16)
    keys_all = keys_all.astype(jnp.bfloat16).reshape(sequences, length_all, features)
    values_all = values_all + value_bias.astype(jnp.float32)
    values_all = values_all.astype(jnp.bfloat16).reshape(sequences, length_all, features)
    query_seqs = queries.reshape(sequences, stretch, features)
    own_segs = lax.dynamic_slice_in_dim(segment_ids, offset, stretch, 1)[:, None, :]
    key_segs = segment_ids[:, :, None]
    place = links.place.astype(jnp.int32).reshape(1)
    attended_seqs, lse_kept = attend(
        place, query_seqs, keys_all, values_all, key_segs, own_segs
    )
    attended_seqs, second_pairs, second_others = lax.optimization_barrier(
        (attended_seqs, second_pairs, second_others)
    )
    full_up, full_down = finish_second(links, second_pairs, second_others)
    attended = attended_seqs.reshape(tokens, features)
    middle = (
        inputs
        + jnp.dot(attended, full_out, preferred_element_type=jnp.float32)
        + out_bias.astype(jnp.float32)
    )
    normed_two = normalize(middle, gain_two, shift_two).astype(jnp.bfloat16)
    pre_act = jnp.concatenate(
        [jnp.dot(normed_two, full_up[j], preferred_element_type=jnp.float32) for j in range(4)],
        axis=1,
    ) + up_bias.astype(jnp.float32)
    hidden = gelu_tanh(pre_act).astype(jnp.bfloat16)
    result = (
        middle
        + jnp.dot(hidden, full_down, preferred_element_type=jnp.float32)
        + down_bias.astype(jnp.float32)
    )
    block_output = result.astype(jnp.bfloat16).reshape(block_input.shape)
    grad_out = cotangent.reshape(tokens, features)
    grad_out_f = grad_out.astype(jnp.float32)
    grad_w_down = contract_rows(hidden, grad_out).astype(jnp.bfloat16)
    grad_b_down = jnp.sum(grad_out_f, axis=0)
    grad_hidden = contract_cols(grad_out, full_down)
    gelu_value, gelu_pull = jax.vjp(gelu_tanh, pre_act)
    grad_pre = gelu_pull(grad_hidden)[0].astype(jnp.bfloat16)
    grads_up = [
        contract_rows(normed_two, grad_pre[:, j * features : (j + 1) * features]).astype(
            jnp.bfloat16
        )
        for j in range(4)
    ]
    down_half = core_rows(links, grad_w_down)
    up_halves = core_halves(links, grads_up)
    grad_b_up = jnp.sum(grad_pre.astype(jnp.float32), axis=0)
    grad_normed_two = sum(
        contract_cols(grad_pre[:, j * features : (j + 1) * features], full_up[j]) for j in range(4)
    )
    norm_value, norm_pull = jax.vjp(normalize, middle, gain_two, shift_two)
    grad_middle_part, grad_gain_two, grad_shift_two = norm_pull(grad_normed_two)
    grad_middle = grad_out_f + grad_middle_part
    grad_middle_low = grad_middle.astype(jnp.bfloat16)
    grad_w_out = contract_rows(attended, grad_middle_low)
    grad_b_out = jnp.sum(grad_middle_low.astype(jnp.float32), axis=0)
    grad_attended = contract_cols(grad_middle_low, full_out).astype(jnp.bfloat16)
    grad_att_seqs = grad_attended.reshape(sequences, stretch, features)

    grad_att_seqs, up_halves, down_half = lax.optimization_barrier(
        (grad_att_seqs, up_halves, down_half)
    )
    second_sums = reduce_second(links, up_halves, down_half)
    grad_queries, key_parts, value_parts = attend_grads(
        place,
        query_seqs,
        keys_all,
        values_all,
        grad_att_seqs,
        attended_seqs,
        lse_kept,
        key_segs,
        own_segs,
    )
    grad_queries = grad_queries.reshape(tokens, features)
    key_rows = key_parts.reshape(-1, features)
    value_rows = value_parts.reshape(-1, features)
    parts = jnp.stack([key_parts, value_parts])
    parts = parts.reshape(2, sequences, links.places, stretch, features).transpose(2, 0, 1, 3, 4)
    own_parts = reduce_stretches(links, parts)
    grad_keys = own_parts[0].reshape(tokens, features)
    grad_values = own_parts[1].reshape(tokens, features)
    grads_first = [
        grad.astype(jnp.bfloat16)
        for grad in (
            contract_rows(normed, grad_queries),
            contract_rows(normed_all, key_rows),
            contract_rows(normed_all, value_rows),
            grad_w_out,
        )
    ]
    first_sums = reduce_first(links, grads_first)
    grad_b_query = jnp.sum(grad_queries.astype(jnp.float32), axis=0)
    grad_b_value = jnp.sum(value_rows.astype(jnp.float32), axis=0)
    grad_normed = (
        contract_cols(grad_queries, full_first[0])
        + contract_cols(grad_keys, full_first[1])
        + contract_cols(grad_values, full_first[2])
    )
    first_value, first_pull = jax.vjp(normalize, inputs, gain_one, shift_one)
    grad_input_part, grad_gain_one, grad_shift_one = first_pull(grad_normed)
    input_grad = (grad_middle + grad_input_part).reshape(block_input.shape)
    vectors = (
        grad_gain_one,
        grad_shift_one,
        grad_b_query,
        grad_b_value,
        grad_b_out,
        grad_gain_two,
        grad_shift_two,
        grad_b_down,
        grad_b_up,
    )
    vector_sums = sum_everywhere(links, jnp.concatenate(vectors))
    mine, start = [], 0
    for vector in vectors:
        size = vector.shape[0]
        own = size // links.shards
        mine.append(lax.dynamic_slice_in_dim(vector_sums, start + links.shard * own, own, 0))
        start += size
    up_sum, down_sum = second_sums[0], second_sums[1]
    return (
        block_output,
        input_grad,
        mine[0],
        mine[1],
        jnp.concatenate([first_sums[j] for j in range(3)], axis=1),
        mine[2],
        mine[3],
        first_sums[3],
        mine[4],
        mine[5],
        mine[6],
        jnp.concatenate([up_sum[j] for j in range(4)], axis=1),
        mine[8],
        down_sum.reshape(-1, features),
        mine[7],
    )


def solution(mesh):
    in_specs = (
        P("fsdp", "context", None),
        P("fsdp", None),
        P("fsdp"),
        P("fsdp"),
        P("fsdp", None),
        P("fsdp"),
        P("fsdp"),
        P("fsdp", None),
        P("fsdp"),
        P("fsdp"),
        P("fsdp"),
        P("fsdp", None),
        P("fsdp"),
        P("fsdp", None),
        P("fsdp"),
        P("fsdp", "context", None),
    )
    out_specs = (
        P("fsdp", "context", None),
        P("fsdp", "context", None),
        P("fsdp"),
        P("fsdp"),
        P("fsdp", None),
        P("fsdp"),
        P("fsdp"),
        P("fsdp", None),
        P("fsdp"),
        P("fsdp"),
        P("fsdp"),
        P("fsdp", None),
        P("fsdp"),
        P("fsdp", None),
        P("fsdp"),
    )
    return jax.shard_map(local, mesh=mesh, in_specs=in_specs, out_specs=out_specs, check_vma=False)
```
